32 devices in a mesh: ax: 4 (over x, core), az: 8 (over z, y).
Axes of the slice: x: 2, y: 2, z: 4, core: 2. Of those that a mesh axis runs over, the one named last changes fastest.
Arguments:
- enthalpy: float32 [16, 1024, 256], P('ax', 'az'), may hold values from -2 to 2.5
- melting_status: int32 [16, 1024, 256], P('ax', 'az'), may hold values from 0 to 2
- plastic_flags: int32 [16, 1024, 256], P('ax', 'az'), may hold values 0 or 1
- displacement: float32 [2, 16, 1024, 256], P(None, 'ax', 'az'), may hold values from -3 to 3
Outputs:
- final_enthalpy: float32 [16, 1024, 256], P('ax', 'az')
- final_displacement: float32 [2, 16, 1024, 256], P(None, 'ax', 'az')
The draws below stay inside these ranges and needn't reach their ends.
All inputs are finite; a program needn't handle non-finite values. No bound on the sum of `plastic_flags` on one device may be relied on, other than what follows from the above.
Results may differ from the reference program's by a relative error of at most 0.0003.
Values sent between devices are 32-bit elements; how exact they have to be, the bound alone decides.
A program may use at most 64 MiB of HBM per device.

```python
import jax
import jax.numpy as jnp
from jax import lax

NR = 256
HEAT_SWEEPS = 3
MECH_SWEEPS = 2
NP = 16
NA = 1024


def plant(values, rng, smallest, high):
    longest = values.shape.index(max(values.shape))
    spots = []
    for shift in (0, 1):
        where = [jax.random.randint(jax.random.fold_in(rng, axis), (), 0, length) for axis, length in enumerate(values.shape)]
        where[longest] = (where[longest] + shift) % values.shape[longest]
        spots.append(tuple(where))
    return values.at[spots[0]].set(smallest).at[spots[1]].set(high)


def block_levels(own_key, dims, pieces, smallest, high):
    level, own = 1.0, jax.random.fold_in(own_key, 6)
    for position, blocks in pieces:
        heights = jnp.exp(jax.random.uniform(jax.random.fold_in(own, position), (blocks,), jnp.float32, smallest / len(pieces), high / len(pieces)))
        level = level * jnp.repeat(heights, dims[position] // blocks).reshape([-1 if axis == position else 1 for axis in range(len(dims))])
    return level


def gaussian(own_key, shape, spread, limit, cuts=(), held_as=jnp.bfloat16):
    values = jax.random.normal(own_key, shape, jnp.float32) * spread
    if len(cuts) > 0:
        values = block_levels(own_key, shape, cuts, -0.22, 0.18) * values
    return jnp.clip(values, min=-limit, max=limit).astype(held_as)


def setup_inputs(seed: int = 0) -> dict:
    streams_of = jax.random.split(jax.random.key(seed), 5)
    return {
        "enthalpy": jnp.clip(-2.0 + 4.5 * jax.random.uniform(streams_of[0], (NP, NA, NR), jnp.float32) ** block_levels(streams_of[0], (NP, NA, NR), ((0, 4), (1, 8)), -0.2, 0.2), -2.0, 2.5),
        "melting_status": plant(jax.random.randint(streams_of[1], (NP, NA, NR), 0, 3), jax.random.fold_in(streams_of[1], 1), 0, 2).astype(jnp.int32),
        "plastic_flags": plant((jax.random.randint(streams_of[2], (NP, NA, NR), 0, 2) < 1).astype(jnp.int32), jax.random.fold_in(streams_of[2], 1), 0, 1),
        "displacement": gaussian(streams_of[3], (2, NP, NA, NR), 0.5, 3.0, ((1, 4), (2, 8)), jnp.float32),
    }


def voxel_kelvin(specific_energy_value, melting_status):
    slope = jnp.where(melting_status == 0, 1.0, jnp.where(melting_status == 1, 0.08, 0.5))
    offset = jnp.where(melting_status == 0, -1.0, jnp.where(melting_status == 1, -0.02, 0.0))
    return slope * specific_energy_value + offset

def conduct(stored_energy_array):
    return 1.0 + 0.6 * jax.nn.sigmoid(-4.0 * stored_energy_array)

def stiffness(stored_energy_array):
    return 1.0 + 3.0 * jax.nn.sigmoid(-3.0 * stored_energy_array)

def worldwide_adjacent_values(field, is_temp):
    zero_plane = jnp.zeros_like(field[:, :1])
    plane_low = jnp.concatenate([zero_plane, field[:, :-1]], axis=1)
    plane_high = jnp.concatenate([field[:, 1:], zero_plane], axis=1)
    if is_temp:
        low_edge = field[..., :1]
        high_edge = field[..., -1:]
    else:
        low_edge = jnp.zeros_like(field[..., :1])
        high_edge = jnp.zeros_like(field[..., :1])
    radial_low = jnp.concatenate([low_edge, field[..., :-1]], axis=3)
    radial_high = jnp.concatenate([field[..., 1:], high_edge], axis=3)
    azim_low = jnp.roll(field, 1, axis=2)
    azim_high = jnp.roll(field, -1, axis=2)
    return [plane_low, plane_high, radial_low, radial_high, azim_low, azim_high]

def heat_neighbours(stored_energy_array):
    zero_plane = jnp.zeros_like(stored_energy_array[:, :1])
    plane_low = jnp.concatenate([zero_plane, stored_energy_array[:, :-1]], axis=1)
    plane_high = jnp.concatenate([stored_energy_array[:, 1:], zero_plane], axis=1)
    inner = jnp.full_like(stored_energy_array[..., :1], -2.0)
    radial_low = jnp.concatenate([inner, stored_energy_array[..., :-1]], axis=3)
    radial_high = jnp.concatenate([stored_energy_array[..., 1:], stored_energy_array[..., -1:]], axis=3)
    return [plane_low, plane_high, radial_low, radial_high, jnp.roll(stored_energy_array, 1, axis=2), jnp.roll(stored_energy_array, -1, axis=2)]

def mechanics(stored_energy_array, creep_rate, disp_field, neighbour_fn):
    temp_near = neighbour_fn(stored_energy_array, True)
    modulus = stiffness(stored_energy_array)
    face_coef = [0.5 * (modulus + stiffness(near)) for near in temp_near]
    diagonal_total = 0.5 + sum(face_coef)
    body_force = jnp.concatenate([0.5 * modulus * 0.5 * (temp_near[3] - temp_near[2]), 0.5 * modulus * 0.5 * (temp_near[5] - temp_near[4])], axis=0)
    yield_stress = 0.3 + 0.5 * jax.nn.sigmoid(-3.0 * stored_energy_array)
    for sweep_index in range(MECH_SWEEPS):
        disp_near = neighbour_fn(disp_field, False)
        strain = jnp.concatenate([0.5 * (disp_near[3][0:1] - disp_near[2][0:1]), 0.5 * (disp_near[5][1:2] - disp_near[4][1:2])], axis=0)
        magnitude = jnp.sqrt(lax.optimization_barrier(jnp.sum(strain * strain, axis=0, keepdims=True)))
        overstress = jnp.maximum(modulus * magnitude - yield_stress, 0.0)
        plastic = creep_rate * overstress / (1.0 + creep_rate * modulus)
        correction = modulus * plastic * strain / jnp.maximum(magnitude, 0.1)
        adjacent_accumulated = sum((coef * near for coef, near in zip(face_coef, disp_near)))
        disp_field = (body_force + adjacent_accumulated - correction) / diagonal_total
    return disp_field

def reference(enthalpy, melting_status, plastic_flags, displacement):
    specific_energy_value = enthalpy[None]
    freeze_status_spread = melting_status[None]
    for sweep_index in range(HEAT_SWEEPS):
        stored_energy_array = voxel_kelvin(specific_energy_value, freeze_status_spread)
        local_heat_conductance = conduct(stored_energy_array)
        flux = sum((0.5 * (local_heat_conductance + conduct(near)) * (near - stored_energy_array) for near in heat_neighbours(stored_energy_array)))
        specific_energy_value = specific_energy_value + 0.08 * flux
    stored_energy_array = voxel_kelvin(specific_energy_value, freeze_status_spread)
    creep_rate = plastic_flags[None].astype(jnp.float32) * 0.6 * jnp.exp(8.0 / 12.0 - 8.0 / (stored_energy_array + 12.0))
    disp_out = mechanics(stored_energy_array, creep_rate, displacement, worldwide_adjacent_values)
    return (specific_energy_value[0], disp_out)
```

```python
import functools
import math

import jax
import jax.numpy as jnp
from jax import lax
from jax.experimental import pallas as pl
from jax.experimental.pallas import tpu as pltpu
from jax.sharding import PartitionSpec as P

HEAT_SWEEPS = 3
SUB = 8
LANE = 128
CHUNKS = 4
PIPES = -2.0
MESH = pl.DeviceIdType.MESH


def weight(t):
    return 0.052 - 0.012 * jnp.tanh(2.0 * t)


def stiffness(t):
    return 2.5 - 1.5 * jnp.tanh(1.5 * t)


def kernel(
    n_ax, n_az, planes, groups,
    h_ref, st_ref, fl_ref, u_ref, h_out, u_out,
    h_raw, st_raw, fl_raw, u_raw, ho_raw, uo_raw,
    T, W, S, H, U, C, row_out, row_in,
    in_sem, out_sem, ax_send, ax_recv, az_send, az_recv,
):
    J = groups
    halves = h_raw.shape[1]
    ax = lax.axis_index("ax")
    az = lax.axis_index("az")
    has_lo = ax > 0
    has_hi = ax < n_ax - 1
    ax_lo, ax_hi = ax - 1, ax + 1
    az_lo = lax.rem(az + n_az - 1, n_az)
    az_hi = lax.rem(az + 1, n_az)

    def whole_in(idx, ref, raw):
        lead = (slice(None),) * (len(ref.shape) - 1)
        return [
            pltpu.make_async_copy(
                ref.at[lead + (pl.ds(q * LANE, LANE),)],
                raw.at[(slice(None),) * (len(ref.shape) - 2) + (q,)],
                in_sem.at[idx, q],
            )
            for q in range(halves)
        ]

    ins = [
        whole_in(i, ref, raw)
        for i, (ref, raw) in enumerate(
            ((h_ref, h_raw), (st_ref, st_raw), (u_ref, u_raw), (fl_ref, fl_raw))
        )
    ]
    for group in ins:
        for copy in group:
            copy.start()

    barrier = pltpu.get_barrier_semaphore()
    pl.semaphore_signal(barrier, inc=1, device_id=(ax, az_lo), device_id_type=MESH)
    pl.semaphore_signal(barrier, inc=1, device_id=(ax, az_hi), device_id_type=MESH)

    @pl.when(has_lo)
    def _():
        pl.semaphore_signal(barrier, inc=1, device_id=(ax_lo, az), device_id_type=MESH)

    @pl.when(has_hi)
    def _():
        pl.semaphore_signal(barrier, inc=1, device_id=(ax_hi, az), device_id_type=MESH)

    def clear(plane):
        def body(j, carry):
            zero = jnp.zeros((SUB, halves * LANE), jnp.float32)
            for k in range(HEAT_SWEEPS + 1):
                T[k, plane, j] = zero
            for m in range(2):
                for c in range(2):
                    U[m, c, plane, j] = zero
            return carry

        lax.fori_loop(1, J + 1, body, 0)

    @pl.when(jnp.logical_not(has_lo))
    def _():
        clear(0)

    @pl.when(jnp.logical_not(has_hi))
    def _():
        clear(planes + 1)

    row_out[...] = jnp.zeros_like(row_out)

    pl.semaphore_wait(barrier, 2 + has_lo.astype(jnp.int32) + has_hi.astype(jnp.int32))

    step = J // CHUNKS
    order = [(c + 1) % CHUNKS for c in range(CHUNKS)]
    NT = HEAT_SWEEPS + 1

    def ax_copy(k, side, c):
        src_plane, dst_plane = (1, planes + 1) if side == 0 else (planes, 0)
        spot = pl.ds(1 + c * step, step)
        if k < NT:
            src, dst = T.at[k, src_plane, spot], T.at[k, dst_plane, spot]
        else:
            src, dst = U.at[k - NT, :, src_plane, spot], U.at[k - NT, :, dst_plane, spot]
        return pltpu.make_async_remote_copy(
            src_ref=src, dst_ref=dst,
            send_sem=ax_send.at[k, side, c], recv_sem=ax_recv.at[k, side, c],
            device_id=(ax_lo if side == 0 else ax_hi, az), device_id_type=MESH,
        )

    def send_ax(k, c):
        @pl.when(has_lo)
        def _():
            ax_copy(k, 0, c).start()

        @pl.when(has_hi)
        def _():
            ax_copy(k, 1, c).start()

    def wait_ax(k, c):
        @pl.when(has_hi)
        def _():
            ax_copy(k, 0, c).wait_recv()

        @pl.when(has_lo)
        def _():
            ax_copy(k, 1, c).wait_recv()

    def az_copy(k, side):
        return pltpu.make_async_remote_copy(
            src_ref=row_out.at[k, side], dst_ref=row_in.at[k, side],
            send_sem=az_send.at[k, side], recv_sem=az_recv.at[k, side],
            device_id=(ax, az_lo if side == 0 else az_hi), device_id_type=MESH,
        )

    def fields(k):
        if k < NT:
            return [(T, (k, p + 1)) for p in range(planes)]
        return [(U, (k - NT, c, p + 1)) for c in range(2) for p in range(planes)]

    def send_az(k, side):
        group, sub = (1, 0) if side == 0 else (J, SUB - 1)
        for i, (ref, at) in enumerate(fields(k)):
            row_out[k, side, i : i + 1, :] = ref[at + (group, pl.ds(sub, 1))]
        az_copy(k, side).start()

    sub_id = lax.broadcasted_iota(jnp.int32, (SUB, halves * LANE), 0)
    lane_id = lax.broadcasted_iota(jnp.int32, (SUB, halves * LANE), 1)
    first_lane = lane_id == 0
    last_lane = lane_id == halves * LANE - 1
    width = halves * LANE

    def wait_az(k, side):
        az_copy(k, side).wait_recv()
        for i, (ref, at) in enumerate(fields(k)):
            row = jnp.broadcast_to(row_in[k, side, i : i + 1, :], (SUB, width))
            if side == 1:
                value = jnp.where(sub_id == 0, row, pltpu.roll(ref[at + (J,)], 1, axis=0))
                spot = at + (0,)
            else:
                value = jnp.where(sub_id == SUB - 1, row, pltpu.roll(ref[at + (1,)], SUB - 1, axis=0))
                spot = at + (J + 1,)
            ref[spot] = value
            if k < NT:
                W[spot] = weight(value) if k < HEAT_SWEEPS else stiffness(value)

    def to_high(x):
        return pltpu.roll(x, width - 1, axis=1)

    def to_low(x):
        return pltpu.roll(x, 1, axis=1)

    def strided(ref, lead, j):
        return jnp.concatenate(
            [ref[lead + (q, pl.ds(j - 1, SUB, stride=J))] for q in range(halves)], axis=1
        )

    def put_strided(ref, lead, j, value):
        for q in range(halves):
            ref[lead + (q, pl.ds(j - 1, SUB, stride=J))] = value[:, q * LANE : (q + 1) * LANE]

    def sends(k, c):
        send_ax(k, c)
        if c == 0:
            send_az(k, 0)
        if c == CHUNKS - 1:
            send_az(k, 1)

    def waits(k, c):
        wait_ax(k, c)
        if c == 0:
            wait_az(k, 1)
        if c == CHUNKS - 1:
            wait_az(k, 0)

    for copy in ins[0] + ins[1]:
        copy.wait()

    def first_temperature(j, carry):
        for p in range(planes):
            h = strided(h_raw, (p,), j)
            st = strided(st_raw, (p,), j)
            s = jnp.where(st == 0, 1.0, jnp.where(st == 1, 0.08, 0.5))
            o = jnp.where(st == 0, -1.0, jnp.where(st == 1, -0.02, 0.0))
            t = s * h + o
            T[0, p + 1, j] = t
            W[0, p + 1, j] = weight(t)
            S[p, j] = s
            H[p, j] = h
        return carry

    for c in order:
        lax.fori_loop(1 + c * step, 1 + (c + 1) * step, first_temperature, 0)
        sends(0, c)

    for copy in ins[2] + ins[3]:
        copy.wait()

    def first_displacement(j, carry):
        for c in range(2):
            for p in range(planes):
                U[0, c, p + 1, j] = strided(u_raw, (c, p), j)
        return carry

    lax.fori_loop(1, J + 1, first_displacement, 0)

    pipe_weight = 0.052 - 0.012 * math.tanh(2.0 * PIPES)

    def heat(k):
        def az_face(p, j):
            return (W[k, p + 1, j] + W[k, p + 1, j + 1]) * (T[k, p + 1, j + 1] - T[k, p + 1, j])

        def body(j, below):
            above = []
            t_lo = T[k, 0, j]
            w_lo = weight(t_lo)
            t, w = T[k, 1, j], W[k, 1, j]
            face = (w + w_lo) * (t - t_lo)
            for p in range(planes):
                if p < planes - 1:
                    t_hi, w_hi = T[k, p + 2, j], W[k, p + 2, j]
                else:
                    t_hi = T[k, planes + 1, j]
                    w_hi = weight(t_hi)
                next_face = (w + w_hi) * (t_hi - t)
                az_high = az_face(p, j)
                net = (next_face - face) + (az_high - below[p])
                radial = (jnp.where(last_lane, pipe_weight, w) + to_high(w)) * (
                    to_high(t) - jnp.where(last_lane, PIPES, t)
                )
                net = net + (jnp.where(last_lane, 0.0, radial) - to_low(radial))
                h = H[p, j] + net
                new = t + S[p, j] * net
                T[k + 1, p + 1, j] = new
                if k < HEAT_SWEEPS - 1:
                    H[p, j] = h
                    W[k + 1, p + 1, j] = weight(new)
                else:
                    put_strided(ho_raw, (p,), j, h)
                    W[k + 1, p + 1, j] = stiffness(new)
                above.append(az_high)
                face, t, w = next_face, t_hi, w_hi
            return tuple(above)

        for c in order:
            waits(k, c)
            start = 1 + c * step
            below = tuple(az_face(p, start - 1) for p in range(planes))
            lax.fori_loop(start, start + step, body, below)
            sends(k + 1, c)
            if k < 2 and c == order[-1]:
                for d in order[2 * k : 2 * k + 2]:
                    sends(NT, d)

    for k in range(HEAT_SWEEPS):
        heat(k)

    def outs(idx, raw, ref):
        lead = (slice(None),) * (len(ref.shape) - 1)
        return [
            pltpu.make_async_copy(
                raw.at[(slice(None),) * (len(ref.shape) - 2) + (q,)],
                ref.at[lead + (pl.ds(q * LANE, LANE),)],
                out_sem.at[idx, q],
            )
            for q in range(halves)
        ]

    h_copies = outs(0, ho_raw, h_out)
    for copy in h_copies:
        copy.start()

    K = HEAT_SWEEPS

    def mechanics(m):
        def az_coef(p, j):
            return W[K, p + 1, j] + W[K, p + 1, j + 1]

        def body(j, below):
            above = []
            e_lo = stiffness(T[K, 0, j])
            e = W[K, 1, j]
            a_lo = e + e_lo
            for p in range(planes):
                e_hi = W[K, p + 2, j] if p < planes - 1 else stiffness(T[K, planes + 1, j])
                a_hi = e + e_hi
                a_up = az_coef(p, j)
                a_down = below[p]
                r_hi = e + jnp.where(last_lane, e, to_high(e))
                r_lo = e + jnp.where(first_lane, e, to_low(e))
                if m == 0:
                    t = T[K, p + 1, j]
                    inverse = 1.0 / (1.0 + ((a_lo + a_hi) + (a_up + a_down) + (r_hi + r_lo)))
                    half = 0.5 * e
                    f0 = half * (
                        jnp.where(last_lane, t, to_high(t)) - jnp.where(first_lane, t, to_low(t))
                    )
                    f1 = half * (T[K, p + 1, j + 1] - T[K, p + 1, j - 1])
                    flags = strided(fl_raw, (p,), j).astype(jnp.float32)
                    rate = flags * 0.6 * jnp.exp(8.0 / 12.0 - 8.0 / (t + 12.0))
                    er = e * rate
                    flow = er / (1.0 + er)
                    C[0, p, j] = inverse
                    C[1, p, j] = f0
                    C[2, p, j] = f1
                    C[3, p, j] = flow
                else:
                    inverse, f0, f1, flow = (C[i, p, j] for i in range(4))
                u0, u1 = U[m, 0, p + 1, j], U[m, 1, p + 1, j]
                u0_hi = jnp.where(last_lane, 0.0, to_high(u0))
                u0_lo = jnp.where(first_lane, 0.0, to_low(u0))
                u1_hi = jnp.where(last_lane, 0.0, to_high(u1))
                u1_lo = jnp.where(first_lane, 0.0, to_low(u1))
                u1_up, u1_down = U[m, 1, p + 1, j + 1], U[m, 1, p + 1, j - 1]
                d0 = u0_hi - u0_lo
                d1 = u1_up - u1_down
                square = 0.25 * (d0 * d0 + d1 * d1)
                root = lax.rsqrt(jnp.maximum(square, 1e-30))
                over = jnp.maximum(e * (square * root) - (0.3 + (e - 1.0) * (1.0 / 6.0)), 0.0)
                factor = flow * over * jnp.minimum(root, 10.0)
                near0 = (
                    (a_lo * U[m, 0, p, j] + a_hi * U[m, 0, p + 2, j])
                    + (a_up * U[m, 0, p + 1, j + 1] + a_down * U[m, 0, p + 1, j - 1])
                    + (r_hi * u0_hi + r_lo * u0_lo)
                )
                near1 = (
                    (a_lo * U[m, 1, p, j] + a_hi * U[m, 1, p + 2, j])
                    + (a_up * u1_up + a_down * u1_down)
                    + (r_hi * u1_hi + r_lo * u1_lo)
                )
                new0 = (f0 + near0 - factor * d0) * inverse
                new1 = (f1 + near1 - factor * d1) * inverse
                if m == 0:
                    U[1, 0, p + 1, j] = new0
                    U[1, 1, p + 1, j] = new1
                else:
                    put_strided(uo_raw, (0, p), j, new0)
                    put_strided(uo_raw, (1, p), j, new1)
                above.append(a_up)
                a_lo, e = a_hi, e_hi
            return tuple(above)

        for c in order:
            if m == 0:
                waits(K, c)
            waits(NT + m, c)
            start = 1 + c * step
            below = tuple(az_coef(p, start - 1) for p in range(planes))
            lax.fori_loop(start, start + step, body, below)
            if m == 0:
                sends(NT + 1, c)

    mechanics(0)
    mechanics(1)

    u_copies = outs(1, uo_raw, u_out)
    for copy in u_copies:
        copy.start()

    for k in range(NT + 2):
        for side in range(2):
            az_copy(k, side).wait_send()

    @pl.when(has_lo)
    def _():
        for k in range(NT + 2):
            for c in range(CHUNKS):
                ax_copy(k, 0, c).wait_send()

    @pl.when(has_hi)
    def _():
        for k in range(NT + 2):
            for c in range(CHUNKS):
                ax_copy(k, 1, c).wait_send()

    for copy in h_copies + u_copies:
        copy.wait()


def on_device(n_ax, n_az, enthalpy, melting_status, plastic_flags, displacement):
    planes, rows, width = enthalpy.shape
    halves = width // LANE
    groups = rows // SUB
    f32 = jnp.float32
    K = HEAT_SWEEPS
    raw = (planes, halves, rows, LANE)
    padded = (planes + 2, groups + 2, SUB, width)
    inner = (planes, groups + 2, SUB, width)
    any_space = pl.BlockSpec(memory_space=pl.ANY)
    exchanges = K + 3
    return pl.pallas_call(
        functools.partial(kernel, n_ax, n_az, planes, groups),
        out_shape=(
            jax.ShapeDtypeStruct(enthalpy.shape, f32),
            jax.ShapeDtypeStruct(displacement.shape, f32),
        ),
        in_specs=[any_space] * 4,
        out_specs=(any_space, any_space),
        scratch_shapes=[
            pltpu.VMEM(raw, f32),
            pltpu.VMEM(raw, jnp.int32),
            pltpu.VMEM(raw, jnp.int32),
            pltpu.VMEM((2,) + raw, f32),
            pltpu.VMEM(raw, f32),
            pltpu.VMEM((2,) + raw, f32),
            pltpu.VMEM((K + 1,) + padded, f32),
            pltpu.VMEM((K + 1,) + padded, f32),
            pltpu.VMEM(inner, f32),
            pltpu.VMEM(inner, f32),
            pltpu.VMEM((2, 2) + padded, f32),
            pltpu.VMEM((4,) + inner, f32),
            pltpu.VMEM((exchanges, 2, 2 * planes, width), f32),
            pltpu.VMEM((exchanges, 2, 2 * planes, width), f32),
            pltpu.SemaphoreType.DMA((4, halves)),
            pltpu.SemaphoreType.DMA((2, halves)),
            pltpu.SemaphoreType.DMA((exchanges, 2, CHUNKS)),
            pltpu.SemaphoreType.DMA((exchanges, 2, CHUNKS)),
            pltpu.SemaphoreType.DMA((exchanges, 2)),
            pltpu.SemaphoreType.DMA((exchanges, 2)),
        ],
        compiler_params=pltpu.CompilerParams(
            collective_id=0, has_side_effects=True, vmem_limit_bytes=40 * 1024 * 1024
        ),
    )(enthalpy, melting_status, plastic_flags, displacement)


def solution(mesh):
    in_specs = (
        P("ax", "az", None),
        P("ax", "az", None),
        P("ax", "az", None),
        P(None, "ax", "az", None),
    )
    out_specs = (P("ax", "az", None), P(None, "ax", "az", None))
    return jax.shard_map(
        functools.partial(on_device, mesh.shape["ax"], mesh.shape["az"]),
        mesh=mesh, in_specs=in_specs, out_specs=out_specs, check_vma=False,
    )
```

```python
import functools
import math

import jax
import jax.numpy as jnp
from jax import lax
from jax.experimental import pallas as pl
from jax.experimental.pallas import tpu as pltpu
from jax.sharding import PartitionSpec as P

HEAT_SWEEPS = 3
SUB = 8
LANE = 128
CHUNKS = 3
HALO = 8
PIPES = -2.0
MESH = pl.DeviceIdType.MESH


def weight(t):
    return 0.052 - 0.012 * jnp.tanh(2.0 * t)


def stiffness(t):
    return 2.5 - 1.5 * jnp.tanh(1.5 * t)


def kernel(
    n_ax, n_az, planes, groups,
    h_ref, st_ref, fl_ref, u_ref, h_out, u_out,
    h_raw, st_raw, fl_raw, u_raw, ho_raw, uo_raw,
    T, W, S, H, U, C,
    in_sem, out_sem, ax_send, ax_recv, az_send, az_recv,
):
    J = groups
    halves = h_raw.shape[1]
    rows = h_ref.shape[1]
    ax = lax.axis_index("ax")
    az = lax.axis_index("az")
    has_lo = ax > 0
    has_hi = ax < n_ax - 1
    ax_lo, ax_hi = ax - 1, ax + 1
    az_lo = lax.rem(az + n_az - 1, n_az)
    az_hi = lax.rem(az + 1, n_az)

    def whole_in(idx, ref, raw):
        lead = (slice(None),) * (len(ref.shape) - 1)
        return [
            pltpu.make_async_copy(
                ref.at[lead + (pl.ds(q * LANE, LANE),)],
                raw.at[(slice(None),) * (len(ref.shape) - 2) + (q, pl.ds(HALO, rows))],
                in_sem.at[idx, q],
            )
            for q in range(halves)
        ]

    pairs = ((h_ref, h_raw), (st_ref, st_raw), (u_ref, u_raw), (fl_ref, fl_raw))
    ins = [whole_in(i, ref, raw) for i, (ref, raw) in enumerate(pairs)]

    def az_copies(idx, side):
        ref, raw = pairs[idx]
        lead = (slice(None),) * (len(ref.shape) - 2)
        source, target = (0, HALO + rows) if side == 0 else (rows - HALO, 0)
        return [
            pltpu.make_async_remote_copy(
                src_ref=ref.at[lead + (pl.ds(source, HALO), pl.ds(q * LANE, LANE))],
                dst_ref=raw.at[lead + (q, pl.ds(target, HALO))],
                send_sem=az_send.at[idx, side, q], recv_sem=az_recv.at[idx, side, q],
                device_id=(ax, az_lo if side == 0 else az_hi), device_id_type=MESH,
            )
            for q in range(halves)
        ]

    def wait_az(idx):
        for side in range(2):
            for copy in az_copies(idx, side):
                copy.wait_recv()
    for group in ins:
        for copy in group:
            copy.start()

    barrier = pltpu.get_barrier_semaphore()
    pl.semaphore_signal(barrier, inc=1, device_id=(ax, az_lo), device_id_type=MESH)
    pl.semaphore_signal(barrier, inc=1, device_id=(ax, az_hi), device_id_type=MESH)

    @pl.when(has_lo)
    def _():
        pl.semaphore_signal(barrier, inc=1, device_id=(ax_lo, az), device_id_type=MESH)

    @pl.when(has_hi)
    def _():
        pl.semaphore_signal(barrier, inc=1, device_id=(ax_hi, az), device_id_type=MESH)

    def clear(plane):
        def body(j, carry):
            zero = jnp.zeros((SUB, halves * LANE), jnp.float32)
            for k in range(HEAT_SWEEPS + 1):
                T[k, plane, j] = zero
            for m in range(2):
                for c in range(2):
                    U[m, c, plane, j] = zero
            return carry

        lax.fori_loop(1, J + 1, body, 0)

    @pl.when(jnp.logical_not(has_lo))
    def _():
        clear(0)

    @pl.when(jnp.logical_not(has_hi))
    def _():
        clear(planes + 1)

    pl.semaphore_wait(barrier, 2 + has_lo.astype(jnp.int32) + has_hi.astype(jnp.int32))
    for idx in (0, 1):
        for side in range(2):
            for copy in az_copies(idx, side):
                copy.start()

    step = J // CHUNKS
    order = [(c + 1) % CHUNKS for c in range(CHUNKS)]
    NT = HEAT_SWEEPS + 1

    def ax_copy(k, side, c):
        src_plane, dst_plane = (1, planes + 1) if side == 0 else (planes, 0)
        spot = pl.ds(1 + c * step, step)
        if k < NT:
            src, dst = T.at[k, src_plane, spot], T.at[k, dst_plane, spot]
        else:
            src, dst = U.at[k - NT, :, src_plane, spot], U.at[k - NT, :, dst_plane, spot]
        return pltpu.make_async_remote_copy(
            src_ref=src, dst_ref=dst,
            send_sem=ax_send.at[k, side, c], recv_sem=ax_recv.at[k, side, c],
            device_id=(ax_lo if side == 0 else ax_hi, az), device_id_type=MESH,
        )

    def send_ax(k, c):
        @pl.when(has_lo)
        def _():
            ax_copy(k, 0, c).start()

        @pl.when(has_hi)
        def _():
            ax_copy(k, 1, c).start()

    def wait_ax(k, c):
        @pl.when(has_hi)
        def _():
            ax_copy(k, 0, c).wait_recv()

        @pl.when(has_lo)
        def _():
            ax_copy(k, 1, c).wait_recv()

    def fields(k):
        if k < NT:
            return [(T, (k, p + 1)) for p in range(planes)]
        return [(U, (k - NT, c, p + 1)) for c in range(2) for p in range(planes)]

    lane_id = lax.broadcasted_iota(jnp.int32, (SUB, halves * LANE), 1)
    first_lane = lane_id == 0
    last_lane = lane_id == halves * LANE - 1
    width = halves * LANE

    def pad(k):
        for ref, at in fields(k):
            for source, target, turn in ((J, 0, 1), (1, J + 1, SUB - 1)):
                ref[at + (target,)] = pltpu.roll(ref[at + (source,)], turn, axis=0)
                if k < NT:
                    W[at + (target,)] = pltpu.roll(W[at + (source,)], turn, axis=0)

    def to_high(x):
        return pltpu.roll(x, width - 1, axis=1)

    def to_low(x):
        return pltpu.roll(x, 1, axis=1)

    def strided(ref, lead, j):
        return jnp.concatenate(
            [ref[lead + (q, pl.ds(j - 1, SUB, stride=J))] for q in range(halves)], axis=1
        )

    def put_strided(ref, lead, j, value):
        for q in range(halves):
            ref[lead + (q, pl.ds(j - 1, SUB, stride=J))] = value[:, q * LANE : (q + 1) * LANE]

    for copy in ins[0] + ins[1]:
        copy.wait()
    wait_az(0)
    wait_az(1)

    def first_temperature(j, carry):
        for p in range(planes):
            h = strided(h_raw, (p,), j)
            st = strided(st_raw, (p,), j)
            s = jnp.where(st == 0, 1.0, jnp.where(st == 1, 0.08, 0.5))
            o = jnp.where(st == 0, -1.0, jnp.where(st == 1, -0.02, 0.0))
            t = s * h + o
            T[0, p + 1, j] = t
            W[0, p + 1, j] = weight(t)
            S[p, j] = s
            H[p, j] = h
        return carry

    for c in order:
        lax.fori_loop(1 + c * step, 1 + (c + 1) * step, first_temperature, 0)
        send_ax(0, c)

    pad(0)
    for idx in (2, 3):
        for side in range(2):
            for copy in az_copies(idx, side):
                copy.start()
    for copy in ins[2] + ins[3]:
        copy.wait()

    def first_displacement(j, carry):
        for c in range(2):
            for p in range(planes):
                U[0, c, p + 1, j] = strided(u_raw, (c, p), j)
        return carry

    pipe_weight = 0.052 - 0.012 * math.tanh(2.0 * PIPES)

    def heat(k):
        def az_face(p, j):
            return (W[k, p + 1, j] + W[k, p + 1, j + 1]) * (T[k, p + 1, j + 1] - T[k, p + 1, j])

        def body(j, below):
            above = []
            t_lo = T[k, 0, j]
            w_lo = weight(t_lo)
            t, w = T[k, 1, j], W[k, 1, j]
            face = (w + w_lo) * (t - t_lo)
            for p in range(planes):
                if p < planes - 1:
                    t_hi, w_hi = T[k, p + 2, j], W[k, p + 2, j]
                else:
                    t_hi = T[k, planes + 1, j]
                    w_hi = weight(t_hi)
                next_face = (w + w_hi) * (t_hi - t)
                az_high = az_face(p, j)
                net = (next_face - face) + (az_high - below[p])
                radial = (jnp.where(last_lane, pipe_weight, w) + to_high(w)) * (
                    to_high(t) - jnp.where(last_lane, PIPES, t)
                )
                net = net + (jnp.where(last_lane, 0.0, radial) - to_low(radial))
                h = H[p, j] + net
                new = t + S[p, j] * net
                T[k + 1, p + 1, j] = new
                if k < HEAT_SWEEPS - 1:
                    H[p, j] = h
                    W[k + 1, p + 1, j] = weight(new)
                else:
                    put_strided(ho_raw, (p,), j, h)
                    W[k + 1, p + 1, j] = stiffness(new)
                above.append(az_high)
                face, t, w = next_face, t_hi, w_hi
            return tuple(above)

        for c in order:
            wait_ax(k, c)
            start = 1 + c * step
            below = tuple(az_face(p, start - 1) for p in range(planes))
            lax.fori_loop(start, start + step, body, below, unroll=2)
            send_ax(k + 1, c)

    for k in range(HEAT_SWEEPS):
        heat(k)
        pad(k + 1)
        if k == 0:
            wait_az(2)
            lax.fori_loop(1, J + 1, first_displacement, 0)
            pad(NT)
            for c in order:
                send_ax(NT, c)
    wait_az(3)

    def outs(idx, raw, ref):
        lead = (slice(None),) * (len(ref.shape) - 1)
        return [
            pltpu.make_async_copy(
                raw.at[(slice(None),) * (len(ref.shape) - 2) + (q, pl.ds(HALO, rows))],
                ref.at[lead + (pl.ds(q * LANE, LANE),)],
                out_sem.at[idx, q],
            )
            for q in range(halves)
        ]

    h_copies = outs(0, ho_raw, h_out)
    for copy in h_copies:
        copy.start()

    K = HEAT_SWEEPS

    def mechanics(m):
        def az_coef(p, j):
            return W[K, p + 1, j] + W[K, p + 1, j + 1]

        def body(j, below):
            above = []
            e_lo = stiffness(T[K, 0, j])
            e = W[K, 1, j]
            a_lo = e + e_lo
            for p in range(planes):
                e_hi = W[K, p + 2, j] if p < planes - 1 else stiffness(T[K, planes + 1, j])
                a_hi = e + e_hi
                a_up = az_coef(p, j)
                a_down = below[p]
                r_hi = e + jnp.where(last_lane, e, to_high(e))
                r_lo = e + jnp.where(first_lane, e, to_low(e))
                if m == 0:
                    t = T[K, p + 1, j]
                    inverse = 1.0 / (1.0 + ((a_lo + a_hi) + (a_up + a_down) + (r_hi + r_lo)))
                    half = 0.5 * e
                    f0 = half * (
                        jnp.where(last_lane, t, to_high(t)) - jnp.where(first_lane, t, to_low(t))
                    )
                    f1 = half * (T[K, p + 1, j + 1] - T[K, p + 1, j - 1])
                    flags = strided(fl_raw, (p,), j).astype(jnp.float32)
                    rate = flags * 0.6 * jnp.exp(8.0 / 12.0 - 8.0 / (t + 12.0))
                    er = e * rate
                    flow = er / (1.0 + er)
                    C[0, p, j] = inverse
                    C[1, p, j] = f0
                    C[2, p, j] = f1
                    C[3, p, j] = flow
                else:
                    inverse, f0, f1, flow = (C[i, p, j] for i in range(4))
                u0, u1 = U[m, 0, p + 1, j], U[m, 1, p + 1, j]
                u0_hi = jnp.where(last_lane, 0.0, to_high(u0))
                u0_lo = jnp.where(first_lane, 0.0, to_low(u0))
                u1_hi = jnp.where(last_lane, 0.0, to_high(u1))
                u1_lo = jnp.where(first_lane, 0.0, to_low(u1))
                u1_up, u1_down = U[m, 1, p + 1, j + 1], U[m, 1, p + 1, j - 1]
                d0 = u0_hi - u0_lo
                d1 = u1_up - u1_down
                square = 0.25 * (d0 * d0 + d1 * d1)
                root = lax.rsqrt(jnp.maximum(square, 1e-30))
                over = jnp.maximum(e * (square * root) - (0.3 + (e - 1.0) * (1.0 / 6.0)), 0.0)
                factor = flow * over * jnp.minimum(root, 10.0)
                near0 = (
                    (a_lo * U[m, 0, p, j] + a_hi * U[m, 0, p + 2, j])
                    + (a_up * U[m, 0, p + 1, j + 1] + a_down * U[m, 0, p + 1, j - 1])
                    + (r_hi * u0_hi + r_lo * u0_lo)
                )
                near1 = (
                    (a_lo * U[m, 1, p, j] + a_hi * U[m, 1, p + 2, j])
                    + (a_up * u1_up + a_down * u1_down)
                    + (r_hi * u1_hi + r_lo * u1_lo)
                )
                new0 = (f0 + near0 - factor * d0) * inverse
                new1 = (f1 + near1 - factor * d1) * inverse
                if m == 0:
                    U[1, 0, p + 1, j] = new0
                    U[1, 1, p + 1, j] = new1
                else:
                    put_strided(uo_raw, (0, p), j, new0)
                    put_strided(uo_raw, (1, p), j, new1)
                above.append(a_up)
                a_lo, e = a_hi, e_hi
            return tuple(above)

        for c in order:
            if m == 0:
                wait_ax(K, c)
            wait_ax(NT + m, c)
            start = 1 + c * step
            below = tuple(az_coef(p, start - 1) for p in range(planes))
            lax.fori_loop(start, start + step, body, below, unroll=2)
            if m == 0:
                send_ax(NT + 1, c)

    mechanics(0)
    pad(NT + 1)
    mechanics(1)

    u_copies = outs(1, uo_raw, u_out)
    for copy in u_copies:
        copy.start()

    for idx in range(4):
        for side in range(2):
            for copy in az_copies(idx, side):
                copy.wait_send()

    @pl.when(has_lo)
    def _():
        for k in range(NT + 2):
            for c in range(CHUNKS):
                ax_copy(k, 0, c).wait_send()

    @pl.when(has_hi)
    def _():
        for k in range(NT + 2):
            for c in range(CHUNKS):
                ax_copy(k, 1, c).wait_send()

    for copy in h_copies + u_copies:
        copy.wait()


def on_device(n_ax, n_az, enthalpy, melting_status, plastic_flags, displacement):
    planes, rows, width = enthalpy.shape
    halves = width // LANE
    groups = (rows + 2 * HALO) // SUB
    f32 = jnp.float32
    K = HEAT_SWEEPS
    raw = (planes, halves, rows + 2 * HALO, LANE)
    padded = (planes + 2, groups + 2, SUB, width)
    inner = (planes, groups + 2, SUB, width)
    any_space = pl.BlockSpec(memory_space=pl.ANY)
    exchanges = K + 3
    return pl.pallas_call(
        functools.partial(kernel, n_ax, n_az, planes, groups),
        out_shape=(
            jax.ShapeDtypeStruct(enthalpy.shape, f32),
            jax.ShapeDtypeStruct(displacement.shape, f32),
        ),
        in_specs=[any_space] * 4,
        out_specs=(any_space, any_space),
        scratch_shapes=[
            pltpu.VMEM(raw, f32),
            pltpu.VMEM(raw, jnp.int32),
            pltpu.VMEM(raw, jnp.int32),
            pltpu.VMEM((2,) + raw, f32),
            pltpu.VMEM(raw, f32),
            pltpu.VMEM((2,) + raw, f32),
            pltpu.VMEM((K + 1,) + padded, f32),
            pltpu.VMEM((K + 1,) + padded, f32),
            pltpu.VMEM(inner, f32),
            pltpu.VMEM(inner, f32),
            pltpu.VMEM((2, 2) + padded, f32),
            pltpu.VMEM((4,) + inner, f32),
            pltpu.SemaphoreType.DMA((4, halves)),
            pltpu.SemaphoreType.DMA((2, halves)),
            pltpu.SemaphoreType.DMA((exchanges, 2, CHUNKS)),
            pltpu.SemaphoreType.DMA((exchanges, 2, CHUNKS)),
            pltpu.SemaphoreType.DMA((4, 2, halves)),
            pltpu.SemaphoreType.DMA((4, 2, halves)),
        ],
        compiler_params=pltpu.CompilerParams(
            collective_id=0, has_side_effects=True, vmem_limit_bytes=60 * 1024 * 1024
        ),
    )(enthalpy, melting_status, plastic_flags, displacement)


def solution(mesh):
    in_specs = (
        P("ax", "az", None),
        P("ax", "az", None),
        P("ax", "az", None),
        P(None, "ax", "az", None),
    )
    out_specs = (P("ax", "az", None), P(None, "ax", "az", None))
    return jax.shard_map(
        functools.partial(on_device, mesh.shape["ax"], mesh.shape["az"]),
        mesh=mesh, in_specs=in_specs, out_specs=out_specs, check_vma=False,
    )
```

```python
import functools
import math

import jax
import jax.numpy as jnp
from jax import lax
from jax.experimental import pallas as pl
from jax.experimental.pallas import tpu as pltpu
from jax.sharding import PartitionSpec as P

HEAT_SWEEPS = 3
MECH_SWEEPS = 2
SUB = 8
LANE = 128
CHUNKS = 3
HALO = 8
REACH = (HEAT_SWEEPS + MECH_SWEEPS, HEAT_SWEEPS + MECH_SWEEPS, MECH_SWEEPS, MECH_SWEEPS - 1)
PIPES = -2.0
MESH = pl.DeviceIdType.MESH


def weight(t):
    return 0.052 - 0.012 * jnp.tanh(2.0 * t)


def stiffness(t):
    return 2.5 - 1.5 * jnp.tanh(1.5 * t)


def kernel(
    n_ax, n_az, planes, groups,
    h_ref, st_ref, fl_ref, u_ref, h_out, u_out,
    h_raw, st_raw, fl_raw, u_raw, ho_raw, uo_raw,
    T, W, S, H, U, C,
    in_sem, out_sem, ax_send, ax_recv, az_send, az_recv,
):
    J = groups
    halves = h_raw.shape[1]
    rows = h_ref.shape[1]
    ax = lax.axis_index("ax")
    az = lax.axis_index("az")
    has_lo = ax > 0
    has_hi = ax < n_ax - 1
    ax_lo, ax_hi = ax - 1, ax + 1
    az_lo = lax.rem(az + n_az - 1, n_az)
    az_hi = lax.rem(az + 1, n_az)

    def whole_in(idx, ref, raw):
        lead = (slice(None),) * (len(ref.shape) - 1)
        return [
            pltpu.make_async_copy(
                ref.at[lead + (pl.ds(q * LANE, LANE),)],
                raw.at[(slice(None),) * (len(ref.shape) - 2) + (q, pl.ds(HALO, rows))],
                in_sem.at[idx, q],
            )
            for q in range(halves)
        ]

    pairs = ((h_ref, h_raw), (st_ref, st_raw), (u_ref, u_raw), (fl_ref, fl_raw))
    ins = [whole_in(i, ref, raw) for i, (ref, raw) in enumerate(pairs)]

    def az_copies(idx, side):
        ref, raw = pairs[idx]
        lead = (slice(None),) * (len(ref.shape) - 2)
        reach = REACH[idx]
        source, target = (0, HALO + rows) if side == 0 else (rows - reach, HALO - reach)
        return [
            pltpu.make_async_remote_copy(
                src_ref=ref.at[lead + (pl.ds(source, reach), pl.ds(q * LANE, LANE))],
                dst_ref=raw.at[lead + (q, pl.ds(target, reach))],
                send_sem=az_send.at[idx, side, q], recv_sem=az_recv.at[idx, side, q],
                device_id=(ax, az_lo if side == 0 else az_hi), device_id_type=MESH,
            )
            for q in range(halves)
        ]

    def wait_az(idx):
        for side in range(2):
            for copy in az_copies(idx, side):
                copy.wait_recv()
    for group in ins:
        for copy in group:
            copy.start()

    for ref, raw in pairs:
        for lead in ((c, p) for c in range(2) for p in range(planes)) if len(raw.shape) == 5 else (
            (p,) for p in range(planes)
        ):
            for q in range(halves):
                for start in (0, HALO + rows):
                    raw[lead + (q, pl.ds(start, HALO))] = jnp.zeros((HALO, LANE), raw.dtype)

    barrier = pltpu.get_barrier_semaphore()
    pl.semaphore_signal(barrier, inc=1, device_id=(ax, az_lo), device_id_type=MESH)
    pl.semaphore_signal(barrier, inc=1, device_id=(ax, az_hi), device_id_type=MESH)

    @pl.when(has_lo)
    def _():
        pl.semaphore_signal(barrier, inc=1, device_id=(ax_lo, az), device_id_type=MESH)

    @pl.when(has_hi)
    def _():
        pl.semaphore_signal(barrier, inc=1, device_id=(ax_hi, az), device_id_type=MESH)

    def clear(plane):
        def body(j, carry):
            zero = jnp.zeros((SUB, halves * LANE), jnp.float32)
            for k in range(HEAT_SWEEPS + 1):
                T[k, plane, j] = zero
            for m in range(2):
                for c in range(2):
                    U[m, c, plane, j] = zero
            return carry

        lax.fori_loop(1, J + 1, body, 0)

    @pl.when(jnp.logical_not(has_lo))
    def _():
        clear(0)

    @pl.when(jnp.logical_not(has_hi))
    def _():
        clear(planes + 1)

    pl.semaphore_wait(barrier, 2 + has_lo.astype(jnp.int32) + has_hi.astype(jnp.int32))
    for idx in range(4):
        for side in range(2):
            for copy in az_copies(idx, side):
                copy.start()

    step = J // CHUNKS
    order = [(c + 1) % CHUNKS for c in range(CHUNKS)]
    NT = HEAT_SWEEPS + 1

    def ax_copy(k, side, c):
        src_plane, dst_plane = (1, planes + 1) if side == 0 else (planes, 0)
        spot = pl.ds(1 + c * step, step)
        if k < NT:
            src, dst = T.at[k, src_plane, spot], T.at[k, dst_plane, spot]
        else:
            src, dst = U.at[k - NT, :, src_plane, spot], U.at[k - NT, :, dst_plane, spot]
        return pltpu.make_async_remote_copy(
            src_ref=src, dst_ref=dst,
            send_sem=ax_send.at[k, side, c], recv_sem=ax_recv.at[k, side, c],
            device_id=(ax_lo if side == 0 else ax_hi, az), device_id_type=MESH,
        )

    def send_ax(k, c):
        @pl.when(has_lo)
        def _():
            ax_copy(k, 0, c).start()

        @pl.when(has_hi)
        def _():
            ax_copy(k, 1, c).start()

    def wait_ax(k, c):
        @pl.when(has_hi)
        def _():
            ax_copy(k, 0, c).wait_recv()

        @pl.when(has_lo)
        def _():
            ax_copy(k, 1, c).wait_recv()

    def fields(k):
        if k < NT:
            return [(T, (k, p + 1)) for p in range(planes)]
        return [(U, (k - NT, c, p + 1)) for c in range(2) for p in range(planes)]

    lane_id = lax.broadcasted_iota(jnp.int32, (SUB, halves * LANE), 1)
    first_lane = lane_id == 0
    last_lane = lane_id == halves * LANE - 1
    width = halves * LANE

    def pad(k):
        for ref, at in fields(k):
            for source, target, turn in ((J, 0, 1), (1, J + 1, SUB - 1)):
                ref[at + (target,)] = pltpu.roll(ref[at + (source,)], turn, axis=0)
                if k < NT:
                    W[at + (target,)] = pltpu.roll(W[at + (source,)], turn, axis=0)

    def to_high(x):
        return pltpu.roll(x, width - 1, axis=1)

    def to_low(x):
        return pltpu.roll(x, 1, axis=1)

    def strided(ref, lead, j):
        return jnp.concatenate(
            [ref[lead + (q, pl.ds(j - 1, SUB, stride=J))] for q in range(halves)], axis=1
        )

    def put_strided(ref, lead, j, value):
        for q in range(halves):
            ref[lead + (q, pl.ds(j - 1, SUB, stride=J))] = value[:, q * LANE : (q + 1) * LANE]

    for copy in ins[0] + ins[1]:
        copy.wait()
    wait_az(0)
    wait_az(1)

    def first_temperature(j, carry):
        for p in range(planes):
            h = strided(h_raw, (p,), j)
            st = strided(st_raw, (p,), j)
            s = jnp.where(st == 0, 1.0, jnp.where(st == 1, 0.08, 0.5))
            o = jnp.where(st == 0, -1.0, jnp.where(st == 1, -0.02, 0.0))
            t = s * h + o
            T[0, p + 1, j] = t
            W[0, p + 1, j] = weight(t)
            S[p, j] = s
            H[p, j] = h
        return carry

    for c in order:
        lax.fori_loop(1 + c * step, 1 + (c + 1) * step, first_temperature, 0)
        send_ax(0, c)

    pad(0)
    for copy in ins[2] + ins[3]:
        copy.wait()
    wait_az(2)

    def first_displacement(j, carry):
        for c in range(2):
            for p in range(planes):
                U[0, c, p + 1, j] = strided(u_raw, (c, p), j)
        return carry

    pipe_weight = 0.052 - 0.012 * math.tanh(2.0 * PIPES)

    def heat(k):
        def az_face(p, j):
            return (W[k, p + 1, j] + W[k, p + 1, j + 1]) * (T[k, p + 1, j + 1] - T[k, p + 1, j])

        def body(j, below):
            above = []
            t_lo = T[k, 0, j]
            w_lo = weight(t_lo)
            t, w = T[k, 1, j], W[k, 1, j]
            face = (w + w_lo) * (t - t_lo)
            for p in range(planes):
                if p < planes - 1:
                    t_hi, w_hi = T[k, p + 2, j], W[k, p + 2, j]
                else:
                    t_hi = T[k, planes + 1, j]
                    w_hi = weight(t_hi)
                next_face = (w + w_hi) * (t_hi - t)
                az_high = az_face(p, j)
                net = (next_face - face) + (az_high - below[p])
                radial = (jnp.where(last_lane, pipe_weight, w) + to_high(w)) * (
                    to_high(t) - jnp.where(last_lane, PIPES, t)
                )
                net = net + (jnp.where(last_lane, 0.0, radial) - to_low(radial))
                h = H[p, j] + net
                new = t + S[p, j] * net
                T[k + 1, p + 1, j] = new
                if k < HEAT_SWEEPS - 1:
                    H[p, j] = h
                    W[k + 1, p + 1, j] = weight(new)
                else:
                    put_strided(ho_raw, (p,), j, h)
                    W[k + 1, p + 1, j] = stiffness(new)
                above.append(az_high)
                face, t, w = next_face, t_hi, w_hi
            return tuple(above)

        for c in order:
            wait_ax(k, c)
            start = 1 + c * step
            below = tuple(az_face(p, start - 1) for p in range(planes))
            lax.fori_loop(start, start + step, body, below, unroll=3)
            send_ax(k + 1, c)

    lax.fori_loop(1, J + 1, first_displacement, 0)
    pad(NT)
    send_ax(NT, order[0])
    for k in range(HEAT_SWEEPS):
        heat(k)
        pad(k + 1)
        if k < HEAT_SWEEPS - 1:
            send_ax(NT, order[k + 1])
    wait_az(3)

    def outs(idx, raw, ref):
        lead = (slice(None),) * (len(ref.shape) - 1)
        return [
            pltpu.make_async_copy(
                raw.at[(slice(None),) * (len(ref.shape) - 2) + (q, pl.ds(HALO, rows))],
                ref.at[(slice(None),) * (len(ref.shape) - 2) + (slice(None), pl.ds(q * LANE, LANE))],
                out_sem.at[idx, q],
            )
            for q in range(halves)
        ]

    h_copies = outs(0, ho_raw, h_out)
    for copy in h_copies:
        copy.start()

    K = HEAT_SWEEPS

    def mechanics(m):
        def az_coef(p, j):
            return W[K, p + 1, j] + W[K, p + 1, j + 1]

        def body(j, below):
            above = []
            e_lo = stiffness(T[K, 0, j])
            e = W[K, 1, j]
            a_lo = e + e_lo
            for p in range(planes):
                e_hi = W[K, p + 2, j] if p < planes - 1 else stiffness(T[K, planes + 1, j])
                a_hi = e + e_hi
                a_up = az_coef(p, j)
                a_down = below[p]
                r_hi = e + jnp.where(last_lane, e, to_high(e))
                r_lo = e + jnp.where(first_lane, e, to_low(e))
                if m == 0:
                    t = T[K, p + 1, j]
                    inverse = 1.0 / (1.0 + ((a_lo + a_hi) + (a_up + a_down) + (r_hi + r_lo)))
                    half = 0.5 * e
                    f0 = half * (
                        jnp.where(last_lane, t, to_high(t)) - jnp.where(first_lane, t, to_low(t))
                    )
                    f1 = half * (T[K, p + 1, j + 1] - T[K, p + 1, j - 1])
                    flags = strided(fl_raw, (p,), j).astype(jnp.float32)
                    rate = flags * 0.6 * jnp.exp(8.0 / 12.0 - 8.0 / (t + 12.0))
                    er = e * rate
                    flow = er / (1.0 + er)
                    C[0, p, j] = inverse
                    C[1, p, j] = f0
                    C[2, p, j] = f1
                    C[3, p, j] = flow
                else:
                    inverse, f0, f1, flow = (C[i, p, j] for i in range(4))
                u0, u1 = U[m, 0, p + 1, j], U[m, 1, p + 1, j]
                u0_hi = jnp.where(last_lane, 0.0, to_high(u0))
                u0_lo = jnp.where(first_lane, 0.0, to_low(u0))
                u1_hi = jnp.where(last_lane, 0.0, to_high(u1))
                u1_lo = jnp.where(first_lane, 0.0, to_low(u1))
                u1_up, u1_down = U[m, 1, p + 1, j + 1], U[m, 1, p + 1, j - 1]
                d0 = u0_hi - u0_lo
                d1 = u1_up - u1_down
                square = 0.25 * (d0 * d0 + d1 * d1)
                root = lax.rsqrt(jnp.maximum(square, 1e-30))
                over = jnp.maximum(e * (square * root) - (0.3 + (e - 1.0) * (1.0 / 6.0)), 0.0)
                factor = flow * over * jnp.minimum(root, 10.0)
                near0 = (
                    (a_lo * U[m, 0, p, j] + a_hi * U[m, 0, p + 2, j])
                    + (a_up * U[m, 0, p + 1, j + 1] + a_down * U[m, 0, p + 1, j - 1])
                    + (r_hi * u0_hi + r_lo * u0_lo)
                )
                near1 = (
                    (a_lo * U[m, 1, p, j] + a_hi * U[m, 1, p + 2, j])
                    + (a_up * u1_up + a_down * u1_down)
                    + (r_hi * u1_hi + r_lo * u1_lo)
                )
                new0 = (f0 + near0 - factor * d0) * inverse
                new1 = (f1 + near1 - factor * d1) * inverse
                if m == 0:
                    U[1, 0, p + 1, j] = new0
                    U[1, 1, p + 1, j] = new1
                else:
                    put_strided(uo_raw, (0, p), j, new0)
                    put_strided(uo_raw, (1, p), j, new1)
                above.append(a_up)
                a_lo, e = a_hi, e_hi
            return tuple(above)

        for c in order:
            if m == 0:
                wait_ax(K, c)
            wait_ax(NT + m, c)
            start = 1 + c * step
            below = tuple(az_coef(p, start - 1) for p in range(planes))
            lax.fori_loop(start, start + step, body, below, unroll=3)
            if m == 0:
                send_ax(NT + 1, c)

    mechanics(0)
    pad(NT + 1)
    mechanics(1)

    u_copies = outs(1, uo_raw, u_out)
    for copy in u_copies:
        copy.start()

    for idx in range(4):
        for side in range(2):
            for copy in az_copies(idx, side):
                copy.wait_send()

    @pl.when(has_lo)
    def _():
        for k in range(NT + 2):
            for c in range(CHUNKS):
                ax_copy(k, 0, c).wait_send()

    @pl.when(has_hi)
    def _():
        for k in range(NT + 2):
            for c in range(CHUNKS):
                ax_copy(k, 1, c).wait_send()

    for copy in h_copies + u_copies:
        copy.wait()


def hand_on(h_in, u_in, h_out, u_out, h_held, u_held, in_sem, out_sem):
    planes = h_in.shape[0]
    parts = [(h_in, h_held, h_out, (p,)) for p in range(planes)]
    parts += [(u_in, u_held, u_out, (c, p)) for c in range(2) for p in range(planes)]
    fetches = [
        pltpu.make_async_copy(source.at[at], held.at[at], in_sem.at[i])
        for i, (source, held, target, at) in enumerate(parts)
    ]
    writes = [
        pltpu.make_async_copy(held.at[at], target.at[at], out_sem.at[i])
        for i, (source, held, target, at) in enumerate(parts)
    ]
    for fetch in fetches:
        fetch.start()
    for fetch, write in zip(fetches, writes):
        fetch.wait()
        write.start()
    for write in writes:
        write.wait()


def on_device(n_ax, n_az, enthalpy, melting_status, plastic_flags, displacement):
    planes, rows, width = enthalpy.shape
    halves = width // LANE
    groups = (rows + 2 * HALO) // SUB
    f32 = jnp.float32
    K = HEAT_SWEEPS
    raw = (planes, halves, rows + 2 * HALO, LANE)
    padded = (planes + 2, groups + 2, SUB, width)
    inner = (planes, groups + 2, SUB, width)
    any_space = pl.BlockSpec(memory_space=pl.ANY)
    exchanges = K + 3
    out_shape = (
        jax.ShapeDtypeStruct(enthalpy.shape, f32),
        jax.ShapeDtypeStruct(displacement.shape, f32),
    )
    results = pl.pallas_call(
        functools.partial(kernel, n_ax, n_az, planes, groups),
        out_shape=out_shape,
        in_specs=[any_space] * 4,
        out_specs=(any_space, any_space),
        scratch_shapes=[
            pltpu.VMEM(raw, f32),
            pltpu.VMEM(raw, jnp.int32),
            pltpu.VMEM(raw, jnp.int32),
            pltpu.VMEM((2,) + raw, f32),
            pltpu.VMEM(raw, f32),
            pltpu.VMEM((2,) + raw, f32),
            pltpu.VMEM((K + 1,) + padded, f32),
            pltpu.VMEM((K + 1,) + padded, f32),
            pltpu.VMEM(inner, f32),
            pltpu.VMEM(inner, f32),
            pltpu.VMEM((2, 2) + padded, f32),
            pltpu.VMEM((4,) + inner, f32),
            pltpu.SemaphoreType.DMA((4, halves)),
            pltpu.SemaphoreType.DMA((2, halves)),
            pltpu.SemaphoreType.DMA((exchanges, 2, CHUNKS)),
            pltpu.SemaphoreType.DMA((exchanges, 2, CHUNKS)),
            pltpu.SemaphoreType.DMA((4, 2, halves)),
            pltpu.SemaphoreType.DMA((4, 2, halves)),
        ],
        compiler_params=pltpu.CompilerParams(
            collective_id=0, has_side_effects=True, vmem_limit_bytes=60 * 1024 * 1024
        ),
    )(enthalpy, melting_status, plastic_flags, displacement)
    return pl.pallas_call(
        hand_on,
        out_shape=out_shape,
        in_specs=[any_space] * 2,
        out_specs=(any_space, any_space),
        scratch_shapes=[
            pltpu.VMEM(enthalpy.shape, f32),
            pltpu.VMEM(displacement.shape, f32),
            pltpu.SemaphoreType.DMA((3 * planes,)),
            pltpu.SemaphoreType.DMA((3 * planes,)),
        ],
    )(*results)


def solution(mesh):
    in_specs = (
        P("ax", "az", None),
        P("ax", "az", None),
        P("ax", "az", None),
        P(None, "ax", "az", None),
    )
    out_specs = (P("ax", "az", None), P(None, "ax", "az", None))
    return jax.shard_map(
        functools.partial(on_device, mesh.shape["ax"], mesh.shape["az"]),
        mesh=mesh, in_specs=in_specs, out_specs=out_specs, check_vma=False,
    )
```
